256 devices in a mesh: param: 16 (over z_hi, y), sensor: 16 (over x, z_lo, core).
Axes of the slice: x: 4, y: 4, z: 8 (z_hi: 4, z_lo: 2; z = z_hi * 2 + z_lo), core: 2. Of those that a mesh axis runs over, the one named last changes fastest.
Arguments:
- seafloor_motion: float32 [420, 65536], P(None, ('param', 'sensor')), may hold values from -6 to 6
- response_blocks: bfloat16 [16, 2, 640, 65536], P(None, None, 'sensor', 'param'), may hold values from -0.25 to 0.25
- frequencies: int32 [16], replicated, may hold values from 0 to 210
- station_of_row: int32 [640], P('sensor'), may hold values from 0 to 639, each once
- noise_precision: float32 [640], replicated, may hold values from 0.2 to 2
Outputs:
- hessian_action: float32 [420, 65536], P(None, ('param', 'sensor'))
The draws below stay inside these ranges and needn't reach their ends.
Inputs may be any that keep to these rules, and one draw needn't show every extreme that they name: `station_of_row`: each station appears in exactly one sensor row. `frequencies`: frequency numbers may repeat.
All inputs are finite; a program needn't handle non-finite values.
Results may differ from the reference program's by a relative error of at most 0.004.
Values may be sent and summed in bfloat16 or wider, within the bound.
No kernel may reach another device: no remote copies, remote signals or barrier semaphores. Data moves between devices by JAX's collectives and lax.ppermute only.
A program may use at most 64 MiB of HBM per device.

```python
import math
import jax
import jax.numpy as jnp
from jax import lax

NT = 420
S = 640
NF = 16
M = 65536


def set_ends(drawn, rng, smallest, high):
    shape = drawn.shape
    spot = [jax.random.randint(jax.random.fold_in(rng, axis), (), 0, shape[axis]) for axis in range(len(shape))]
    drawn = drawn.at[tuple(spot)].set(smallest)
    longest = shape.index(max(shape))
    spot[longest] = (spot[longest] + 1) % shape[longest]
    return drawn.at[tuple(spot)].set(high)


def raised(entries, stream_key, source, target, shards_of, factor):
    def block_of(axis_at):
        return (jnp.arange(entries.shape[axis_at]) // (entries.shape[axis_at] // shards_of)).reshape((-1,) + (1,) * (entries.ndim - 1 - axis_at))

    one_side = jax.random.permutation(stream_key, shards_of)[block_of(target)]
    far = (block_of(target) + shards_of // 2) % shards_of
    return jnp.where((block_of(source) == one_side) | (block_of(source) == far), factor * entries, entries)


def shard_levels(rng, dims, cuts, smallest, top_value):
    def one(dim, parts):
        heights = jax.random.uniform(jax.random.fold_in(jax.random.fold_in(rng, 6), dim), (parts,), jnp.float32, smallest / len(cuts), top_value / len(cuts))
        return jnp.repeat(jnp.exp(heights), dims[dim] // parts).reshape((-1,) + (1,) * (len(dims) - dim - 1))

    factor_of = one(*cuts[0])
    for cut in cuts[1:]:
        factor_of = factor_of * one(*cut)
    return factor_of


def normal_values(key, extent, scale, most, pieces=(), kind=jnp.bfloat16):
    factor_of = shard_levels(key, extent, pieces, -0.22, 0.18) if pieces else 1.0
    array = jax.random.normal(key, extent, jnp.float32) * scale * factor_of
    return jnp.minimum(jnp.maximum(array, -most), most).astype(kind)


def bell_draw_with(rng, extent, scale, most, cuts, heavy, kind=jnp.bfloat16):
    array = scale * jax.random.normal(rng, extent, jnp.float32)
    if cuts:
        array = array * shard_levels(rng, extent, cuts, -0.22, 0.18)
    return jnp.clip(raised(array, jax.random.fold_in(rng, 3), *heavy), -most, most).astype(kind)


def setup_inputs(seed: int = 0) -> dict:
    splits = jax.random.split(jax.random.key(seed), 6)
    return {
        "seafloor_motion": normal_values(splits[0], (NT, M), 1.0, 6.0, ((1, 256),), jnp.float32),
        "response_blocks": bell_draw_with(splits[1], (NF, 2, S, M), (2 * S) ** -0.5, 0.25, ((2, 16), (3, 16)), (2, 3, 16, 2.0)),
        "frequencies": set_ends(jax.random.randint(splits[2], (NF,), 0, NT // 2 + 1), jax.random.fold_in(splits[2], 1), 0, (NT // 2 + 1) - 1).astype(jnp.int32),
        "station_of_row": jax.random.permutation(splits[3], S).astype(jnp.int32),
        "noise_precision": jnp.clip(jnp.exp(jax.random.uniform(splits[4], (S,), jnp.float32, math.log(0.2), math.log(2.0))), 0.2, 2.0),
    }


def reference(seafloor_motion, response_blocks, frequencies, station_of_row, noise_precision):
    highest = lax.Precision.HIGHEST
    steps = jnp.arange(NT, dtype=jnp.int32)
    phase = frequencies.astype(jnp.int32)[:, None] * steps[None, :] % NT
    angle = phase.astype(jnp.float32) * (2.0 * math.pi / NT)
    scale = 1.0 / math.sqrt(NT)
    cosine_table = jnp.cos(angle) * scale
    sine_table = jnp.sin(angle) * scale
    spec_real = jnp.dot(cosine_table, seafloor_motion, precision=highest)
    spec_imag = -jnp.dot(sine_table, seafloor_motion, precision=highest)
    spectrum = jnp.stack([spec_real, spec_imag], axis=1).astype(jnp.bfloat16)

    def forward(items):
        block, spec = items
        block = block.astype(jnp.float32)
        spec = spec.astype(jnp.float32)
        real_block, imag_block = (block[0], block[1])
        data_real = jnp.dot(real_block, spec[0], precision=highest) - jnp.dot(imag_block, spec[1], precision=highest)
        data_imag = jnp.dot(real_block, spec[1], precision=highest) + jnp.dot(imag_block, spec[0], precision=highest)
        return jnp.stack([data_real, data_imag], axis=0)
    data = lax.map(forward, (response_blocks, spectrum))
    weight = noise_precision[station_of_row]
    weighted = (data * weight[None, None, :]).astype(jnp.bfloat16)

    def backward(items):
        block, wdata = items
        block = block.astype(jnp.float32)
        wdata = wdata.astype(jnp.float32)
        real_block, imag_block = (block[0], block[1])
        adj_real = jnp.dot(wdata[0], real_block, precision=highest) + jnp.dot(wdata[1], imag_block, precision=highest)
        adj_imag = jnp.dot(wdata[1], real_block, precision=highest) - jnp.dot(wdata[0], imag_block, precision=highest)
        return jnp.stack([adj_real, adj_imag], axis=0)
    adjoint = lax.map(backward, (response_blocks, weighted))
    return jnp.dot(cosine_table.T, adjoint[:, 0], precision=highest) - jnp.dot(sine_table.T, adjoint[:, 1], precision=highest)
```

```python
import functools
import math

import jax
import jax.numpy as jnp
from jax import lax
from jax.experimental import pallas as pl
from jax.experimental.pallas import tpu as pltpu
from jax.sharding import PartitionSpec as P

F32 = jnp.float32
BF16 = jnp.bfloat16
VMEM = pl.BlockSpec(memory_space=pltpu.VMEM)
SIN_TERMS = (-1.0 / 6, 1.0 / 120, -1.0 / 5040, 1.0 / 362880, -1.0 / 39916800)
COS_TERMS = (-1.0 / 2, 1.0 / 24, -1.0 / 720, 1.0 / 40320, -1.0 / 3628800, 1.0 / 479001600)


def series(square, terms):
    total = jnp.full_like(square, terms[-1])
    for term in terms[-2::-1]:
        total = total * square + term
    return total


def trig_tables(frequency, step, num_steps):
    turns = (frequency * step).astype(F32)
    rest = turns - num_steps * jnp.floor(turns * (1.0 / num_steps))
    rest = jnp.where(rest < 0, rest + num_steps, rest)
    rest = jnp.where(rest >= num_steps, rest - num_steps, rest)
    rest = jnp.where(rest > num_steps / 2, rest - num_steps, rest)
    flip = jnp.abs(rest) > num_steps / 4
    near = jnp.where(flip, jnp.where(rest > 0, num_steps / 2, -num_steps / 2) - rest, rest)
    angle = near * (2.0 * math.pi / num_steps)
    square = angle * angle
    scale = 1.0 / math.sqrt(num_steps)
    cosine = (1.0 + square * series(square, COS_TERMS)) * jnp.where(flip, -scale, scale)
    sine = (angle + angle * square * series(square, SIN_TERMS)) * scale
    return cosine, sine


def split3(value):
    high = value.astype(BF16)
    rest = value - high.astype(F32)
    middle = rest.astype(BF16)
    low = (rest - middle.astype(F32)).astype(BF16)
    return high, middle, low


def dot(a, b, dims):
    return lax.dot_general(a, b, (dims, ((), ())), preferred_element_type=F32)


def table_of(frequencies_ref, num_freq, num_steps):
    frequency = frequencies_ref[...]
    step = lax.broadcasted_iota(jnp.int32, (num_freq, num_steps), 1)
    cosine, sine = trig_tables(frequency, step, num_steps)
    return jnp.concatenate([cosine, -sine], axis=0)


def spectrum_kernel(frequencies_ref, motion_ref, out_ref):
    num_freq = frequencies_ref.shape[0]
    num_steps = motion_ref.shape[0]
    rows = 2 * num_freq
    table = jnp.concatenate(split3(table_of(frequencies_ref, num_freq, num_steps)), axis=0)
    high, middle, low = split3(motion_ref[...])
    nn = ((1,), (0,))
    by_high = dot(table, high, nn)
    by_middle = dot(table[: 2 * rows], middle, nn)
    by_low = dot(table[:rows], low, nn)
    spectrum = (
        by_high[2 * rows :] + by_middle[rows:] + by_low + by_high[rows : 2 * rows] + by_middle[:rows]
    ) + by_high[:rows]
    out_ref[...] = jnp.broadcast_to(spectrum.astype(BF16)[None], out_ref.shape)


def swap_parts(row, sensors):
    lanes = row.shape[1]
    lane = lax.broadcasted_iota(jnp.int32, row.shape, 1)
    first = lax.rem(lane, 2 * sensors) < sensors
    return jnp.where(first, pltpu.roll(row, lanes - sensors, 1), pltpu.roll(row, sensors, 1)), first


def own_frequency(num_freq, lanes):
    freq = lax.broadcasted_iota(jnp.int32, (num_freq, lanes), 0)
    lane = lax.broadcasted_iota(jnp.int32, (num_freq, lanes), 1)
    each = lanes // num_freq
    return (lane >= freq * each) & (lane < (freq + 1) * each)


def forward_kernel(sensors, num_freq, spectrum_ref, blocks_ref, out_ref):
    pieces, _, width = spectrum_ref.shape
    lanes = blocks_ref.shape[0]
    total = jnp.zeros((2 * num_freq, lanes), F32)
    for piece in range(pieces):
        part = blocks_ref[:, piece * width : (piece + 1) * width]
        total += dot(spectrum_ref[piece], part, ((1,), (1,)))
    own = own_frequency(num_freq, lanes)
    by_real = jnp.sum(jnp.where(own, total[:num_freq], 0.0), axis=0, keepdims=True)
    by_imag = jnp.sum(jnp.where(own, total[num_freq:], 0.0), axis=0, keepdims=True)
    by_real = jnp.broadcast_to(by_real, (8, lanes))
    by_imag = jnp.broadcast_to(by_imag, (8, lanes))
    swapped, first = swap_parts(by_imag, sensors)
    data = by_real + jnp.where(first, -swapped, swapped)
    for piece in range(out_ref.shape[0]):
        out_ref[piece] = data[:1]


def backward_kernel(sensors, num_freq, data_ref, weight_ref, blocks_ref, out_ref):
    lanes = blocks_ref.shape[0]
    pieces, rows, width = out_ref.shape
    data = jnp.sum(data_ref[...], axis=0)
    weighted = jnp.broadcast_to(data * weight_ref[...], (8, lanes)).astype(BF16).astype(F32)
    swapped, first = swap_parts(weighted, sensors)
    turned = jnp.where(first, swapped, -swapped)
    own = own_frequency(num_freq, lanes)
    left = jnp.concatenate(
        [jnp.where(own, weighted[:1], 0.0), jnp.where(own, turned[:1], 0.0)], axis=0
    ).astype(BF16)
    for piece in range(pieces):
        part = blocks_ref[:, piece * width : (piece + 1) * width]
        out_ref[piece] = dot(left, part, ((1,), (0,))).astype(BF16)


def final_kernel(frequencies_ref, adjoint_ref, out_ref):
    num_freq = frequencies_ref.shape[0]
    num_steps = out_ref.shape[0]
    adjoint = jnp.sum(adjoint_ref[...].astype(F32), axis=0)
    th, tm, tl = split3(table_of(frequencies_ref, num_freq, num_steps))
    ah, am, al = split3(adjoint)
    left = jnp.concatenate([tl, tm, th, tm, th, th], axis=0)
    right = jnp.concatenate([ah, am, al, ah, am, ah], axis=0)
    out_ref[...] = dot(left, right, ((0,), (0,)))


def call(kernel, shape, dtype, args, limit):
    return pl.pallas_call(
        kernel,
        out_shape=jax.ShapeDtypeStruct(shape, dtype),
        in_specs=[VMEM] * len(args),
        out_specs=VMEM,
        compiler_params=pltpu.CompilerParams(vmem_limit_bytes=limit),
    )(*args)


def per_device(seafloor_motion, response_blocks, frequencies, station_of_row, noise_precision):
    num_freq, _, sensors, params = response_blocks.shape
    num_steps, width = seafloor_motion.shape
    rows = 2 * num_freq
    lanes = rows * sensors
    pieces = params // width
    blocks = response_blocks.reshape(lanes, params)
    column = frequencies[:, None]

    matches = station_of_row[:, None] == jnp.arange(noise_precision.shape[0], dtype=jnp.int32)[None, :]
    weight = jnp.sum(jnp.where(matches, noise_precision[None, :], 0.0), axis=1)
    weight = jnp.tile(weight, rows)[None]

    copies = call(
        spectrum_kernel, (pieces, rows, width), BF16, (column, seafloor_motion), 16 << 20
    )
    spectrum = lax.all_to_all(copies, "sensor", 0, 0)
    partial = call(
        functools.partial(forward_kernel, sensors, num_freq),
        (lax.axis_size("param"), 1, lanes),
        F32,
        (spectrum, blocks),
        16 << 20,
    )
    data = lax.all_to_all(partial, "param", 0, 0)
    pieces_out = call(
        functools.partial(backward_kernel, sensors, num_freq),
        (pieces, rows, width),
        BF16,
        (data, weight, blocks),
        16 << 20,
    )
    adjoint = lax.all_to_all(pieces_out, "sensor", 0, 0)
    return call(final_kernel, (num_steps, width), F32, (column, adjoint), 16 << 20)


def solution(mesh):
    in_specs = (
        P(None, ("param", "sensor")),
        P(None, None, "sensor", "param"),
        P(),
        P("sensor"),
        P(),
    )
    return jax.shard_map(
        per_device,
        mesh=mesh,
        in_specs=in_specs,
        out_specs=P(None, ("param", "sensor")),
        check_vma=False,
    )
```

```python
import functools
import math

import jax
import jax.numpy as jnp
from jax import lax
from jax.experimental import pallas as pl
from jax.experimental.pallas import tpu as pltpu
from jax.sharding import PartitionSpec as P

F32 = jnp.float32
BF16 = jnp.bfloat16
VMEM = pl.BlockSpec(memory_space=pltpu.VMEM)
HBM = pl.BlockSpec(memory_space=pltpu.HBM)
SIN_TERMS = (-1.0 / 6, 1.0 / 120, -1.0 / 5040, 1.0 / 362880, -1.0 / 39916800)
COS_TERMS = (-1.0 / 2, 1.0 / 24, -1.0 / 720, 1.0 / 40320, -1.0 / 3628800, 1.0 / 479001600)


def series(square, terms):
    total = jnp.full_like(square, terms[-1])
    for term in terms[-2::-1]:
        total = total * square + term
    return total


def trig_tables(frequency, step, num_steps):
    turns = (frequency * step).astype(F32)
    rest = turns - num_steps * jnp.floor(turns * (1.0 / num_steps))
    rest = jnp.where(rest < 0, rest + num_steps, rest)
    rest = jnp.where(rest >= num_steps, rest - num_steps, rest)
    rest = jnp.where(rest > num_steps / 2, rest - num_steps, rest)
    flip = jnp.abs(rest) > num_steps / 4
    near = jnp.where(flip, jnp.where(rest > 0, num_steps / 2, -num_steps / 2) - rest, rest)
    angle = near * (2.0 * math.pi / num_steps)
    square = angle * angle
    scale = 1.0 / math.sqrt(num_steps)
    cosine = (1.0 + square * series(square, COS_TERMS)) * jnp.where(flip, -scale, scale)
    sine = (angle + angle * square * series(square, SIN_TERMS)) * scale
    return cosine, sine


def split3(value):
    high = value.astype(BF16)
    rest = value - high.astype(F32)
    middle = rest.astype(BF16)
    low = (rest - middle.astype(F32)).astype(BF16)
    return high, middle, low


def dot(a, b, dims):
    return lax.dot_general(a, b, (dims, ((), ())), preferred_element_type=F32)


def column_of(row):
    size = row.shape[1]
    across = lax.broadcasted_iota(jnp.int32, (size, size), 1)
    down = lax.broadcasted_iota(jnp.int32, (size, size), 0)
    return jnp.sum(jnp.where(across == down, row, jnp.zeros_like(row)), axis=1, keepdims=True)


def spectrum_kernel(
    frequencies_hbm, motion_hbm, station_hbm, noise_hbm, out_ref, table_ref, weight_ref,
    frequencies_ref, motion_ref, station_ref, noise_ref, sems,
):
    copies = [
        pltpu.make_async_copy(source, target, sems.at[i])
        for i, (source, target) in enumerate(
            [
                (frequencies_hbm, frequencies_ref),
                (station_hbm, station_ref),
                (noise_hbm, noise_ref),
                (motion_hbm, motion_ref),
            ]
        )
    ]
    for copy in copies:
        copy.start()
    num_freq = frequencies_ref.shape[1]
    num_steps = motion_ref.shape[0]
    rows = 2 * num_freq

    copies[0].wait()
    frequency = column_of(frequencies_ref[...])
    step = lax.broadcasted_iota(jnp.int32, (num_freq, num_steps), 1)
    cosine, sine = trig_tables(frequency, step, num_steps)
    table = jnp.concatenate(split3(jnp.concatenate([cosine, -sine], axis=0)), axis=0)
    table_ref[...] = table

    copies[1].wait()
    copies[2].wait()
    sensors, lanes = station_ref.shape[1], weight_ref.shape[1]
    station = column_of(station_ref[...])
    runs, length = noise_ref.shape
    place = lax.broadcasted_iota(jnp.int32, (sensors, length), 1)
    found = jnp.zeros((sensors, length), F32)
    for run in range(runs):
        found += jnp.where(station == place + run * length, noise_ref[run : run + 1], 0.0)
    by_sensor = jnp.sum(found, axis=1, keepdims=True)
    sensor = lax.broadcasted_iota(jnp.int32, (sensors, lanes), 0)
    lane = lax.rem(lax.broadcasted_iota(jnp.int32, (1, lanes), 1), sensors)
    weight_ref[...] = jnp.sum(jnp.where(sensor == lane, by_sensor, 0.0), axis=0, keepdims=True)

    copies[3].wait()
    high, middle, low = split3(motion_ref[...])
    nn = ((1,), (0,))
    by_high = dot(table, high, nn)
    by_middle = dot(table[: 2 * rows], middle, nn)
    by_low = dot(table[:rows], low, nn)
    spectrum = (
        by_high[2 * rows :] + by_middle[rows:] + by_low + by_high[rows : 2 * rows] + by_middle[:rows]
    ) + by_high[:rows]
    out_ref[...] = jnp.broadcast_to(spectrum.astype(BF16)[None], out_ref.shape)


def swap_parts(row, sensors):
    lanes = row.shape[1]
    lane = lax.broadcasted_iota(jnp.int32, row.shape, 1)
    first = lax.rem(lane, 2 * sensors) < sensors
    return jnp.where(first, pltpu.roll(row, lanes - sensors, 1), pltpu.roll(row, sensors, 1)), first


def own_frequency(num_freq, lanes):
    freq = lax.broadcasted_iota(jnp.int32, (num_freq, lanes), 0)
    lane = lax.broadcasted_iota(jnp.int32, (num_freq, lanes), 1)
    each = lanes // num_freq
    return (lane >= freq * each) & (lane < (freq + 1) * each)


def forward_kernel(sensors, num_freq, spectrum_ref, blocks_ref, out_ref):
    pieces = spectrum_ref.shape[0]
    lanes = blocks_ref.shape[0]
    spectrum = jnp.concatenate([spectrum_ref[piece] for piece in range(pieces)], axis=1)
    total = dot(blocks_ref[...], spectrum, ((1,), (1,))).T
    own = own_frequency(num_freq, lanes)
    by_real = jnp.sum(jnp.where(own, total[:num_freq], 0.0), axis=0, keepdims=True)
    by_imag = jnp.sum(jnp.where(own, total[num_freq:], 0.0), axis=0, keepdims=True)
    by_real = jnp.broadcast_to(by_real, (8, lanes))
    by_imag = jnp.broadcast_to(by_imag, (8, lanes))
    swapped, first = swap_parts(by_imag, sensors)
    data = by_real + jnp.where(first, -swapped, swapped)
    for piece in range(out_ref.shape[0]):
        out_ref[piece] = data[:1]


def backward_kernel(sensors, num_freq, data_ref, weight_ref, blocks_ref, out_ref):
    lanes = blocks_ref.shape[0]
    pieces, rows, width = out_ref.shape
    data = jnp.sum(data_ref[...], axis=0)
    weighted = jnp.broadcast_to(data * weight_ref[...], (8, lanes)).astype(BF16).astype(F32)
    swapped, first = swap_parts(weighted, sensors)
    turned = jnp.where(first, swapped, -swapped)
    own = own_frequency(num_freq, lanes)
    left = jnp.concatenate(
        [jnp.where(own, weighted[:1], 0.0), jnp.where(own, turned[:1], 0.0)], axis=0
    ).astype(BF16)
    for piece in range(pieces):
        part = blocks_ref[:, piece * width : (piece + 1) * width]
        out_ref[piece] = dot(left, part, ((1,), (0,))).astype(BF16)


def final_kernel(table_ref, adjoint_ref, out_ref):
    rows = adjoint_ref.shape[1]
    adjoint = jnp.sum(adjoint_ref[...].astype(F32), axis=0)
    table = table_ref[...]
    th, tm, tl = table[:rows], table[rows : 2 * rows], table[2 * rows :]
    ah, am, al = split3(adjoint)
    left = jnp.concatenate([tl, tm, th, tm, th, th], axis=0)
    right = jnp.concatenate([ah, am, al, ah, am, ah], axis=0)
    out_ref[...] = dot(left, right, ((0,), (0,)))


def call(kernel, outs, args, spaces=None, scratch=(), cost=None):
    spaces = spaces or [VMEM] * len(args)
    return pl.pallas_call(
        kernel,
        out_shape=[jax.ShapeDtypeStruct(shape, dtype) for shape, dtype in outs],
        in_specs=spaces,
        out_specs=[VMEM] * len(outs),
        scratch_shapes=scratch,
        compiler_params=pltpu.CompilerParams(vmem_limit_bytes=16 << 20),
        cost_estimate=cost,
    )(*args)


def per_device(seafloor_motion, response_blocks, frequencies, station_of_row, noise_precision):
    num_freq, _, sensors, params = response_blocks.shape
    num_steps, width = seafloor_motion.shape
    rows = 2 * num_freq
    lanes = rows * sensors
    pieces = params // width
    blocks = response_blocks.reshape(lanes, params)
    small = (frequencies[None], seafloor_motion, station_of_row[None], noise_precision.reshape(-1, 128))
    small = tuple(pltpu.with_memory_space_constraint(x, pltpu.HBM) for x in small)
    busy = pl.CostEstimate(flops=20 * 10**9, bytes_accessed=64 << 20, transcendentals=0)

    copies, table, weight = call(
        spectrum_kernel,
        [((pieces, rows, width), BF16), ((3 * rows, num_steps), BF16), ((1, lanes), F32)],
        small,
        [HBM] * len(small),
        [pltpu.VMEM(x.shape, x.dtype) for x in small] + [pltpu.SemaphoreType.DMA((len(small),))],
        busy,
    )
    spectrum = lax.all_to_all(copies, "sensor", 0, 0)
    (partial,) = call(
        functools.partial(forward_kernel, sensors, num_freq),
        [((lax.axis_size("param"), 1, lanes), F32)],
        (spectrum, blocks),
        cost=busy,
    )
    data = lax.all_to_all(partial, "param", 0, 0)
    (pieces_out,) = call(
        functools.partial(backward_kernel, sensors, num_freq),
        [((pieces, rows, width), BF16)],
        (data, weight, blocks),
    )
    adjoint = lax.all_to_all(pieces_out, "sensor", 0, 0)
    return call(final_kernel, [((num_steps, width), F32)], (table, adjoint))[0]


def solution(mesh):
    in_specs = (
        P(None, ("param", "sensor")),
        P(None, None, "sensor", "param"),
        P(),
        P("sensor"),
        P(),
    )
    return jax.shard_map(
        per_device,
        mesh=mesh,
        in_specs=in_specs,
        out_specs=P(None, ("param", "sensor")),
        check_vma=False,
    )
```

```python
import functools
import math

import jax
import jax.numpy as jnp
from jax import lax
from jax.experimental import pallas as pl
from jax.experimental.pallas import tpu as pltpu
from jax.sharding import PartitionSpec as P

F32 = jnp.float32
BF16 = jnp.bfloat16
VMEM = pl.BlockSpec(memory_space=pltpu.VMEM)
HBM = pl.BlockSpec(memory_space=pltpu.HBM)
SIN_TERMS = (-1.0 / 6, 1.0 / 120, -1.0 / 5040, 1.0 / 362880, -1.0 / 39916800)
COS_TERMS = (-1.0 / 2, 1.0 / 24, -1.0 / 720, 1.0 / 40320, -1.0 / 3628800, 1.0 / 479001600)


def series(square, terms):
    total = jnp.full_like(square, terms[-1])
    for term in terms[-2::-1]:
        total = total * square + term
    return total


def trig_tables(frequency, step, num_steps):
    turns = (frequency * step).astype(F32)
    rest = turns - num_steps * jnp.floor(turns * (1.0 / num_steps))
    rest = jnp.where(rest < 0, rest + num_steps, rest)
    rest = jnp.where(rest >= num_steps, rest - num_steps, rest)
    rest = jnp.where(rest > num_steps / 2, rest - num_steps, rest)
    flip = jnp.abs(rest) > num_steps / 4
    near = jnp.where(flip, jnp.where(rest > 0, num_steps / 2, -num_steps / 2) - rest, rest)
    angle = near * (2.0 * math.pi / num_steps)
    square = angle * angle
    scale = 1.0 / math.sqrt(num_steps)
    cosine = (1.0 + square * series(square, COS_TERMS)) * jnp.where(flip, -scale, scale)
    sine = (angle + angle * square * series(square, SIN_TERMS)) * scale
    return cosine, sine


def split3(value):
    high = value.astype(BF16)
    rest = value - high.astype(F32)
    middle = rest.astype(BF16)
    low = (rest - middle.astype(F32)).astype(BF16)
    return high, middle, low


def dot(a, b, dims):
    return lax.dot_general(a, b, (dims, ((), ())), preferred_element_type=F32)


def column_of(row):
    size = row.shape[1]
    across = lax.broadcasted_iota(jnp.int32, (size, size), 1)
    down = lax.broadcasted_iota(jnp.int32, (size, size), 0)
    return jnp.sum(jnp.where(across == down, row, jnp.zeros_like(row)), axis=1, keepdims=True)


def spectrum_kernel(
    frequencies_hbm, motion_hbm, station_hbm, noise_hbm, out_ref, table_ref, weight_ref,
    frequencies_ref, motion_ref, station_ref, noise_ref, sems,
):
    copies = [
        pltpu.make_async_copy(source, target, sems.at[i])
        for i, (source, target) in enumerate(
            [
                (frequencies_hbm, frequencies_ref),
                (station_hbm, station_ref),
                (noise_hbm, noise_ref),
                (motion_hbm, motion_ref),
            ]
        )
    ]
    for copy in copies:
        copy.start()
    num_freq = frequencies_ref.shape[1]
    num_steps = motion_ref.shape[0]
    rows = 2 * num_freq

    copies[0].wait()
    frequency = column_of(frequencies_ref[...])
    step = lax.broadcasted_iota(jnp.int32, (num_freq, num_steps), 1)
    cosine, sine = trig_tables(frequency, step, num_steps)
    table = jnp.concatenate(split3(jnp.concatenate([cosine, -sine], axis=0)), axis=0)
    table_ref[...] = table

    copies[1].wait()
    copies[2].wait()
    sensors, lanes = station_ref.shape[1], weight_ref.shape[1]
    station = column_of(station_ref[...])
    runs, length = noise_ref.shape
    place = lax.broadcasted_iota(jnp.int32, (sensors, length), 1)
    found = jnp.zeros((sensors, length), F32)
    for run in range(runs):
        found += jnp.where(station == place + run * length, noise_ref[run : run + 1], 0.0)
    by_sensor = jnp.sum(found, axis=1, keepdims=True)
    sensor = lax.broadcasted_iota(jnp.int32, (sensors, lanes), 0)
    lane = lax.rem(lax.broadcasted_iota(jnp.int32, (1, lanes), 1), sensors)
    weight_ref[...] = jnp.sum(jnp.where(sensor == lane, by_sensor, 0.0), axis=0, keepdims=True)

    copies[3].wait()
    high, middle, low = split3(motion_ref[...])
    nn = ((1,), (0,))
    by_high = dot(table, high, nn)
    by_middle = dot(table[: 2 * rows], middle, nn)
    by_low = dot(table[:rows], low, nn)
    spectrum = (
        by_high[2 * rows :] + by_middle[rows:] + by_low + by_high[rows : 2 * rows] + by_middle[:rows]
    ) + by_high[:rows]
    out_ref[...] = jnp.broadcast_to(spectrum.astype(BF16)[None], out_ref.shape)


def swap_parts(row, sensors):
    lanes = row.shape[1]
    lane = lax.broadcasted_iota(jnp.int32, row.shape, 1)
    first = lax.rem(lane, 2 * sensors) < sensors
    return jnp.where(first, pltpu.roll(row, lanes - sensors, 1), pltpu.roll(row, sensors, 1)), first


def own_frequency(num_freq, lanes):
    freq = lax.broadcasted_iota(jnp.int32, (num_freq, lanes), 0)
    lane = lax.broadcasted_iota(jnp.int32, (num_freq, lanes), 1)
    each = lanes // num_freq
    return (lane >= freq * each) & (lane < (freq + 1) * each)


def own_core():
    return lax.rem(lax.axis_index("sensor"), 2)


def piece_columns(piece, core, width):
    return pl.ds(pl.multiple_of((2 * piece + core) * width, width), width)


def half_forward(spectrum_ref, blocks_ref, core):
    pieces, _, width = spectrum_ref.shape
    spectrum = jnp.concatenate([spectrum_ref[piece] for piece in range(pieces)], axis=1)
    columns = [blocks_ref[:, piece_columns(piece, core, width)] for piece in range(pieces)]
    return dot(jnp.concatenate(columns, axis=1), spectrum, ((1,), (1,)))


def own_forward_kernel(spectrum_ref, blocks_ref, out_ref):
    out_ref[...] = half_forward(spectrum_ref, blocks_ref, own_core())


def other_forward_kernel(sensors, num_freq, spectrum_ref, own_ref, blocks_ref, out_ref):
    lanes = blocks_ref.shape[0]
    total = (own_ref[...] + half_forward(spectrum_ref, blocks_ref, 1 - own_core())).T
    own = own_frequency(num_freq, lanes)
    by_real = jnp.sum(jnp.where(own, total[:num_freq], 0.0), axis=0, keepdims=True)
    by_imag = jnp.sum(jnp.where(own, total[num_freq:], 0.0), axis=0, keepdims=True)
    by_real = jnp.broadcast_to(by_real, (8, lanes))
    by_imag = jnp.broadcast_to(by_imag, (8, lanes))
    swapped, first = swap_parts(by_imag, sensors)
    data = by_real + jnp.where(first, -swapped, swapped)
    for piece in range(out_ref.shape[0]):
        out_ref[piece] = data[:1]


def other_backward_kernel(sensors, num_freq, data_ref, weight_ref, blocks_ref, out_ref, left_ref):
    lanes = blocks_ref.shape[0]
    pieces, _, width = out_ref.shape
    data = jnp.sum(data_ref[...], axis=0)
    weighted = jnp.broadcast_to(data * weight_ref[...], (8, lanes)).astype(BF16).astype(F32)
    swapped, first = swap_parts(weighted, sensors)
    turned = jnp.where(first, swapped, -swapped)
    own = own_frequency(num_freq, lanes)
    left = jnp.concatenate(
        [jnp.where(own, weighted[:1], 0.0), jnp.where(own, turned[:1], 0.0)], axis=0
    ).astype(BF16)
    left_ref[...] = left
    other = 1 - own_core()
    for piece in range(pieces):
        part = blocks_ref[:, piece_columns(piece, other, width)]
        out_ref[piece] = dot(left, part, ((1,), (0,))).astype(BF16)


def own_backward_kernel(left_ref, blocks_ref, out_ref):
    pieces, _, width = out_ref.shape
    for piece in range(pieces):
        part = blocks_ref[:, piece_columns(piece, own_core(), width)]
        out_ref[piece] = dot(left_ref[...], part, ((1,), (0,)))


def joined_backward_kernel(left_ref, blocks_ref, first_ref, arrived_ref, out_ref):
    done, _, width = first_ref.shape
    pieces = out_ref.shape[0]
    for piece in range(done, pieces):
        part = blocks_ref[:, piece_columns(piece, own_core(), width)]
        product = dot(left_ref[...], part, ((1,), (0,)))
        out_ref[piece] = (product + arrived_ref[piece].astype(F32)).astype(BF16)
    for piece in range(done):
        out_ref[piece] = (first_ref[piece] + arrived_ref[piece].astype(F32)).astype(BF16)


def final_kernel(table_ref, adjoint_ref, out_ref):
    rows = adjoint_ref.shape[1]
    adjoint = jnp.sum(adjoint_ref[...].astype(F32), axis=0)
    table = table_ref[...]
    th, tm, tl = table[:rows], table[rows : 2 * rows], table[2 * rows :]
    ah, am, al = split3(adjoint)
    left = jnp.concatenate([tl, tm, th, tm, th, th], axis=0)
    right = jnp.concatenate([ah, am, al, ah, am, ah], axis=0)
    out_ref[...] = dot(left, right, ((0,), (0,)))


def call(kernel, outs, args, spaces=None, scratch=(), cost=None):
    spaces = spaces or [VMEM] * len(args)
    return pl.pallas_call(
        kernel,
        out_shape=[jax.ShapeDtypeStruct(shape, dtype) for shape, dtype in outs],
        in_specs=spaces,
        out_specs=[VMEM] * len(outs),
        scratch_shapes=scratch,
        compiler_params=pltpu.CompilerParams(vmem_limit_bytes=16 << 20),
        cost_estimate=cost,
    )(*args)


def per_device(seafloor_motion, response_blocks, frequencies, station_of_row, noise_precision):
    num_freq, _, sensors, params = response_blocks.shape
    num_steps, width = seafloor_motion.shape
    rows = 2 * num_freq
    lanes = rows * sensors
    pieces = params // width
    blocks = response_blocks.reshape(lanes, params)
    small = (frequencies[None], seafloor_motion, station_of_row[None], noise_precision.reshape(-1, 128))
    small = tuple(pltpu.with_memory_space_constraint(x, pltpu.HBM) for x in small)
    busy = pl.CostEstimate(flops=20 * 10**9, bytes_accessed=64 << 20, transcendentals=0)
    half = pieces // 2
    cores = [[2 * piece + core for piece in range(half)] for core in range(2)]
    swap = [(device, device ^ 1) for device in range(pieces)]
    ahead = (half * 5) // 8

    copies, table, weight = call(
        spectrum_kernel,
        [((half, rows, width), BF16), ((3 * rows, num_steps), BF16), ((1, lanes), F32)],
        small,
        [HBM] * len(small),
        [pltpu.VMEM(x.shape, x.dtype) for x in small] + [pltpu.SemaphoreType.DMA((len(small),))],
        busy,
    )
    spectrum = lax.all_to_all(copies, "sensor", 0, 0, axis_index_groups=cores)
    other_spectrum = lax.ppermute(spectrum, "sensor", swap)
    (own,) = call(own_forward_kernel, [((lanes, rows), F32)], (spectrum, blocks), cost=busy)
    (partial,) = call(
        functools.partial(other_forward_kernel, sensors, num_freq),
        [((lax.axis_size("param"), 1, lanes), F32)],
        (other_spectrum, own, blocks),
        cost=busy,
    )
    data = lax.all_to_all(partial, "param", 0, 0)
    to_other, left = call(
        functools.partial(other_backward_kernel, sensors, num_freq),
        [((half, rows, width), BF16), ((rows, lanes), BF16)],
        (data, weight, blocks),
        cost=busy,
    )
    arrived = lax.ppermute(to_other, "sensor", swap)
    (first,) = call(own_backward_kernel, [((ahead, rows, width), F32)], (left, blocks), cost=busy)
    (joined,) = call(
        joined_backward_kernel, [((half, rows, width), BF16)], (left, blocks, first, arrived), cost=busy
    )
    adjoint = lax.all_to_all(joined, "sensor", 0, 0, axis_index_groups=cores)
    return call(final_kernel, [((num_steps, width), F32)], (table, adjoint))[0]


def solution(mesh):
    in_specs = (
        P(None, ("param", "sensor")),
        P(None, None, "sensor", "param"),
        P(),
        P("sensor"),
        P(),
    )
    return jax.shard_map(
        per_device,
        mesh=mesh,
        in_specs=in_specs,
        out_specs=P(None, ("param", "sensor")),
        check_vma=False,
    )
```

```python
import functools
import math

import jax
import jax.numpy as jnp
from jax import lax
from jax.experimental import pallas as pl
from jax.experimental.pallas import tpu as pltpu
from jax.sharding import PartitionSpec as P

F32 = jnp.float32
BF16 = jnp.bfloat16
VMEM = pl.BlockSpec(memory_space=pltpu.VMEM)
HBM = pl.BlockSpec(memory_space=pltpu.HBM)
SIN_TERMS = (-1.0 / 6, 1.0 / 120, -1.0 / 5040, 1.0 / 362880, -1.0 / 39916800)
COS_TERMS = (-1.0 / 2, 1.0 / 24, -1.0 / 720, 1.0 / 40320, -1.0 / 3628800, 1.0 / 479001600)


def series(square, terms):
    total = jnp.full_like(square, terms[-1])
    for term in terms[-2::-1]:
        total = total * square + term
    return total


def trig_tables(frequency, step, num_steps):
    turns = (frequency * step).astype(F32)
    rest = turns - num_steps * jnp.floor(turns * (1.0 / num_steps))
    rest = jnp.where(rest < 0, rest + num_steps, rest)
    rest = jnp.where(rest >= num_steps, rest - num_steps, rest)
    rest = jnp.where(rest > num_steps / 2, rest - num_steps, rest)
    flip = jnp.abs(rest) > num_steps / 4
    near = jnp.where(flip, jnp.where(rest > 0, num_steps / 2, -num_steps / 2) - rest, rest)
    angle = near * (2.0 * math.pi / num_steps)
    square = angle * angle
    scale = 1.0 / math.sqrt(num_steps)
    cosine = (1.0 + square * series(square, COS_TERMS)) * jnp.where(flip, -scale, scale)
    sine = (angle + angle * square * series(square, SIN_TERMS)) * scale
    return cosine, sine


def split3(value):
    high = value.astype(BF16)
    rest = value - high.astype(F32)
    middle = rest.astype(BF16)
    low = (rest - middle.astype(F32)).astype(BF16)
    return high, middle, low


def dot(a, b, dims):
    return lax.dot_general(a, b, (dims, ((), ())), preferred_element_type=F32)


def column_of(row):
    size = row.shape[1]
    across = lax.broadcasted_iota(jnp.int32, (size, size), 1)
    down = lax.broadcasted_iota(jnp.int32, (size, size), 0)
    return jnp.sum(jnp.where(across == down, row, jnp.zeros_like(row)), axis=1, keepdims=True)


def spectrum_kernel(
    frequencies_hbm, motion_hbm, station_hbm, noise_hbm, out_ref, table_ref, weight_ref,
    frequencies_ref, motion_ref, station_ref, noise_ref, sems,
):
    copies = [
        pltpu.make_async_copy(source, target, sems.at[i])
        for i, (source, target) in enumerate(
            [
                (frequencies_hbm, frequencies_ref),
                (station_hbm, station_ref),
                (noise_hbm, noise_ref),
                (motion_hbm, motion_ref),
            ]
        )
    ]
    for copy in copies:
        copy.start()
    num_freq = frequencies_ref.shape[1]
    num_steps = motion_ref.shape[0]
    rows = 2 * num_freq

    copies[0].wait()
    frequency = column_of(frequencies_ref[...])
    step = lax.broadcasted_iota(jnp.int32, (num_freq, num_steps), 1)
    cosine, sine = trig_tables(frequency, step, num_steps)
    table = jnp.concatenate(split3(jnp.concatenate([cosine, -sine], axis=0)), axis=0)
    table_ref[...] = table

    copies[1].wait()
    copies[2].wait()
    sensors, lanes = station_ref.shape[1], weight_ref.shape[1]
    station = column_of(station_ref[...])
    runs, length = noise_ref.shape
    place = lax.broadcasted_iota(jnp.int32, (sensors, length), 1)
    found = jnp.zeros((sensors, length), F32)
    for run in range(runs):
        found += jnp.where(station == place + run * length, noise_ref[run : run + 1], 0.0)
    by_sensor = jnp.sum(found, axis=1, keepdims=True)
    sensor = lax.broadcasted_iota(jnp.int32, (sensors, lanes), 0)
    lane = lax.rem(lax.broadcasted_iota(jnp.int32, (1, lanes), 1), sensors)
    weight_ref[...] = jnp.sum(jnp.where(sensor == lane, by_sensor, 0.0), axis=0, keepdims=True)

    copies[3].wait()
    high, middle, low = split3(motion_ref[...])
    nn = ((1,), (0,))
    by_high = dot(table, high, nn)
    by_middle = dot(table[: 2 * rows], middle, nn)
    by_low = dot(table[:rows], low, nn)
    spectrum = (
        by_high[2 * rows :] + by_middle[rows:] + by_low + by_high[rows : 2 * rows] + by_middle[:rows]
    ) + by_high[:rows]
    out_ref[...] = jnp.broadcast_to(spectrum.astype(BF16)[None], out_ref.shape)


def swap_parts(row, sensors):
    lanes = row.shape[1]
    lane = lax.broadcasted_iota(jnp.int32, row.shape, 1)
    first = lax.rem(lane, 2 * sensors) < sensors
    return jnp.where(first, pltpu.roll(row, lanes - sensors, 1), pltpu.roll(row, sensors, 1)), first


def own_frequency(num_freq, lanes):
    freq = lax.broadcasted_iota(jnp.int32, (num_freq, lanes), 0)
    lane = lax.broadcasted_iota(jnp.int32, (num_freq, lanes), 1)
    each = lanes // num_freq
    return (lane >= freq * each) & (lane < (freq + 1) * each)


def own_core():
    return lax.rem(lax.axis_index("sensor"), 2)


def piece_columns(piece, core, width):
    return pl.ds(pl.multiple_of((2 * piece + core) * width, width), width)


def half_forward(spectrum_ref, blocks_ref, core):
    pieces, _, width = spectrum_ref.shape
    spectrum = jnp.concatenate([spectrum_ref[piece] for piece in range(pieces)], axis=1)
    columns = [blocks_ref[:, piece_columns(piece, core, width)] for piece in range(pieces)]
    return dot(jnp.concatenate(columns, axis=1), spectrum, ((1,), (1,)))


def own_forward_kernel(spectrum_ref, blocks_ref, out_ref):
    out_ref[...] = half_forward(spectrum_ref, blocks_ref, own_core())


def other_forward_kernel(sensors, num_freq, spectrum_ref, own_ref, blocks_ref, out_ref):
    lanes = blocks_ref.shape[0]
    total = (own_ref[...] + half_forward(spectrum_ref, blocks_ref, 1 - own_core())).T
    own = own_frequency(num_freq, lanes)
    by_real = jnp.sum(jnp.where(own, total[:num_freq], 0.0), axis=0, keepdims=True)
    by_imag = jnp.sum(jnp.where(own, total[num_freq:], 0.0), axis=0, keepdims=True)
    by_real = jnp.broadcast_to(by_real, (8, lanes))
    by_imag = jnp.broadcast_to(by_imag, (8, lanes))
    swapped, first = swap_parts(by_imag, sensors)
    data = by_real + jnp.where(first, -swapped, swapped)
    for piece in range(out_ref.shape[0]):
        out_ref[piece] = data[:1]


def other_backward_kernel(sensors, num_freq, data_ref, weight_ref, blocks_ref, out_ref, left_ref):
    lanes = blocks_ref.shape[0]
    pieces, _, width = out_ref.shape
    data = jnp.sum(data_ref[...], axis=0)
    weighted = jnp.broadcast_to(data * weight_ref[...], (8, lanes)).astype(BF16).astype(F32)
    swapped, first = swap_parts(weighted, sensors)
    turned = jnp.where(first, swapped, -swapped)
    own = own_frequency(num_freq, lanes)
    left = jnp.concatenate(
        [jnp.where(own, weighted[:1], 0.0), jnp.where(own, turned[:1], 0.0)], axis=0
    ).astype(BF16)
    left_ref[...] = left
    other = 1 - own_core()
    for piece in range(pieces):
        part = blocks_ref[:, piece_columns(piece, other, width)]
        out_ref[piece] = dot(left, part, ((1,), (0,))).astype(BF16)


def own_backward_kernel(left_ref, blocks_ref, out_ref):
    pieces, _, width = out_ref.shape
    for piece in range(pieces):
        part = blocks_ref[:, piece_columns(piece, own_core(), width)]
        out_ref[piece] = dot(left_ref[...], part, ((1,), (0,)))


def joined_kernel(first_ref, arrived_ref, out_ref):
    out_ref[...] = (first_ref[...] + arrived_ref[...].astype(F32)).astype(BF16)


def final_kernel(table_ref, adjoint_ref, out_ref):
    rows = adjoint_ref.shape[1]
    adjoint = jnp.sum(adjoint_ref[...].astype(F32), axis=0)
    table = table_ref[...]
    th, tm, tl = table[:rows], table[rows : 2 * rows], table[2 * rows :]
    ah, am, al = split3(adjoint)
    left = jnp.concatenate([tl, tm, th, tm, th, th], axis=0)
    right = jnp.concatenate([ah, am, al, ah, am, ah], axis=0)
    out_ref[...] = dot(left, right, ((0,), (0,)))


def call(kernel, outs, args, spaces=None, scratch=(), cost=None):
    spaces = spaces or [VMEM] * len(args)
    return pl.pallas_call(
        kernel,
        out_shape=[jax.ShapeDtypeStruct(shape, dtype) for shape, dtype in outs],
        in_specs=spaces,
        out_specs=[VMEM] * len(outs),
        scratch_shapes=scratch,
        compiler_params=pltpu.CompilerParams(vmem_limit_bytes=16 << 20),
        cost_estimate=cost,
    )(*args)


def per_device(seafloor_motion, response_blocks, frequencies, station_of_row, noise_precision):
    num_freq, _, sensors, params = response_blocks.shape
    num_steps, width = seafloor_motion.shape
    rows = 2 * num_freq
    lanes = rows * sensors
    pieces = params // width
    blocks = response_blocks.reshape(lanes, params)
    small = (frequencies[None], seafloor_motion, station_of_row[None], noise_precision.reshape(-1, 128))
    small = tuple(pltpu.with_memory_space_constraint(x, pltpu.HBM) for x in small)
    busy = pl.CostEstimate(flops=20 * 10**9, bytes_accessed=64 << 20, transcendentals=0)
    half = pieces // 2
    cores = [[2 * piece + core for piece in range(half)] for core in range(2)]
    swap = [(device, device ^ 1) for device in range(pieces)]

    copies, table, weight = call(
        spectrum_kernel,
        [((half, rows, width), BF16), ((3 * rows, num_steps), BF16), ((1, lanes), F32)],
        small,
        [HBM] * len(small),
        [pltpu.VMEM(x.shape, x.dtype) for x in small] + [pltpu.SemaphoreType.DMA((len(small),))],
        busy,
    )
    spectrum = lax.all_to_all(copies, "sensor", 0, 0, axis_index_groups=cores)
    other_spectrum = lax.ppermute(spectrum, "sensor", swap)
    (own,) = call(own_forward_kernel, [((lanes, rows), F32)], (spectrum, blocks), cost=busy)
    (partial,) = call(
        functools.partial(other_forward_kernel, sensors, num_freq),
        [((lax.axis_size("param"), 1, lanes), F32)],
        (other_spectrum, own, blocks),
        cost=busy,
    )
    data = lax.all_to_all(partial, "param", 0, 0)
    to_other, left = call(
        functools.partial(other_backward_kernel, sensors, num_freq),
        [((half, rows, width), BF16), ((rows, lanes), BF16)],
        (data, weight, blocks),
        cost=busy,
    )
    arrived = lax.ppermute(to_other, "sensor", swap)
    (first,) = call(own_backward_kernel, [((half, rows, width), F32)], (left, blocks), cost=busy)
    (joined,) = call(joined_kernel, [((half, rows, width), BF16)], (first, arrived), cost=busy)
    adjoint = lax.all_to_all(joined, "sensor", 0, 0, axis_index_groups=cores)
    return call(final_kernel, [((num_steps, width), F32)], (table, adjoint))[0]


def solution(mesh):
    in_specs = (
        P(None, ("param", "sensor")),
        P(None, None, "sensor", "param"),
        P(),
        P("sensor"),
        P(),
    )
    return jax.shard_map(
        per_device,
        mesh=mesh,
        in_specs=in_specs,
        out_specs=P(None, ("param", "sensor")),
        check_vma=False,
    )
```

```python
import functools
import math

import jax
import jax.numpy as jnp
from jax import lax
from jax.experimental import pallas as pl
from jax.experimental.pallas import tpu as pltpu
from jax.sharding import PartitionSpec as P

F32 = jnp.float32
STAGES = ((1,), (3,), (4,), (12,))
PLACES = (0, 5, 2, 7, 4, 1, 6, 3)
BF16 = jnp.bfloat16
VMEM = pl.BlockSpec(memory_space=pltpu.VMEM)
HBM = pl.BlockSpec(memory_space=pltpu.HBM)
SIN_TERMS = (-1.0 / 6, 1.0 / 120, -1.0 / 5040, 1.0 / 362880, -1.0 / 39916800)
COS_TERMS = (-1.0 / 2, 1.0 / 24, -1.0 / 720, 1.0 / 40320, -1.0 / 3628800, 1.0 / 479001600)


def series(square, terms):
    total = jnp.full_like(square, terms[-1])
    for term in terms[-2::-1]:
        total = total * square + term
    return total


def trig_tables(frequency, step, num_steps):
    turns = (frequency * step).astype(F32)
    rest = turns - num_steps * jnp.floor(turns * (1.0 / num_steps))
    rest = jnp.where(rest < 0, rest + num_steps, rest)
    rest = jnp.where(rest >= num_steps, rest - num_steps, rest)
    rest = jnp.where(rest > num_steps / 2, rest - num_steps, rest)
    flip = jnp.abs(rest) > num_steps / 4
    near = jnp.where(flip, jnp.where(rest > 0, num_steps / 2, -num_steps / 2) - rest, rest)
    angle = near * (2.0 * math.pi / num_steps)
    square = angle * angle
    scale = 1.0 / math.sqrt(num_steps)
    cosine = (1.0 + square * series(square, COS_TERMS)) * jnp.where(flip, -scale, scale)
    sine = (angle + angle * square * series(square, SIN_TERMS)) * scale
    return cosine, sine


def split3(value):
    high = value.astype(BF16)
    rest = value - high.astype(F32)
    middle = rest.astype(BF16)
    low = (rest - middle.astype(F32)).astype(BF16)
    return high, middle, low


def dot(a, b, dims):
    return lax.dot_general(a, b, (dims, ((), ())), preferred_element_type=F32)


def column_of(row):
    size = row.shape[1]
    across = lax.broadcasted_iota(jnp.int32, (size, size), 1)
    down = lax.broadcasted_iota(jnp.int32, (size, size), 0)
    return jnp.sum(jnp.where(across == down, row, jnp.zeros_like(row)), axis=1, keepdims=True)


def spectrum_kernel(
    frequencies_hbm, motion_hbm, station_hbm, noise_hbm, out_ref, table_ref, weight_ref,
    frequencies_ref, motion_ref, station_ref, noise_ref, sems,
):
    copies = [
        pltpu.make_async_copy(source, target, sems.at[i])
        for i, (source, target) in enumerate(
            [
                (frequencies_hbm, frequencies_ref),
                (station_hbm, station_ref),
                (noise_hbm, noise_ref),
                (motion_hbm, motion_ref),
            ]
        )
    ]
    for copy in copies:
        copy.start()
    num_freq = frequencies_ref.shape[1]
    num_steps = motion_ref.shape[0]
    rows = 2 * num_freq

    copies[0].wait()
    frequency = column_of(frequencies_ref[...])
    step = lax.broadcasted_iota(jnp.int32, (num_freq, num_steps), 1)
    cosine, sine = trig_tables(frequency, step, num_steps)
    table = jnp.concatenate(split3(jnp.concatenate([cosine, -sine], axis=0)), axis=0)
    table_ref[...] = table

    copies[1].wait()
    copies[2].wait()
    sensors, lanes = station_ref.shape[1], weight_ref.shape[1]
    station = column_of(station_ref[...])
    runs, length = noise_ref.shape
    place = lax.broadcasted_iota(jnp.int32, (sensors, length), 1)
    found = jnp.zeros((sensors, length), F32)
    for run in range(runs):
        found += jnp.where(station == place + run * length, noise_ref[run : run + 1], 0.0)
    by_sensor = jnp.sum(found, axis=1, keepdims=True)
    sensor = lax.broadcasted_iota(jnp.int32, (sensors, lanes), 0)
    lane = lax.rem(lax.broadcasted_iota(jnp.int32, (1, lanes), 1), sensors)
    weight_ref[...] = jnp.sum(jnp.where(sensor == lane, by_sensor, 0.0), axis=0, keepdims=True)

    copies[3].wait()
    high, middle, low = split3(motion_ref[...])
    nn = ((1,), (0,))
    by_high = dot(table, high, nn)
    by_middle = dot(table[: 2 * rows], middle, nn)
    by_low = dot(table[:rows], low, nn)
    spectrum = (
        by_high[2 * rows :] + by_middle[rows:] + by_low + by_high[rows : 2 * rows] + by_middle[:rows]
    ) + by_high[:rows]
    out_ref[...] = jnp.broadcast_to(spectrum.astype(BF16)[None], out_ref.shape)


def swap_parts(row, sensors):
    lanes = row.shape[1]
    lane = lax.broadcasted_iota(jnp.int32, row.shape, 1)
    first = lax.rem(lane, 2 * sensors) < sensors
    return jnp.where(first, pltpu.roll(row, lanes - sensors, 1), pltpu.roll(row, sensors, 1)), first


def own_frequency(num_freq, lanes):
    freq = lax.broadcasted_iota(jnp.int32, (num_freq, lanes), 0)
    lane = lax.broadcasted_iota(jnp.int32, (num_freq, lanes), 1)
    each = lanes // num_freq
    return (lane >= freq * each) & (lane < (freq + 1) * each)


def own_core():
    return lax.rem(lax.axis_index("sensor"), 2)


def piece_columns(piece, core, width):
    return pl.ds(pl.multiple_of((2 * PLACES[piece] + core) * width, width), width)


def half_forward(spectrum_ref, blocks_ref, core):
    pieces, _, width = spectrum_ref.shape
    spectrum = jnp.concatenate([spectrum_ref[piece] for piece in range(pieces)], axis=1)
    columns = [blocks_ref[:, piece_columns(piece, core, width)] for piece in range(pieces)]
    return dot(jnp.concatenate(columns, axis=1), spectrum, ((1,), (1,)))


def own_forward_kernel(spectrum_ref, blocks_ref, out_ref):
    out_ref[...] = half_forward(spectrum_ref, blocks_ref, own_core())


def other_forward_kernel(sensors, num_freq, spectrum_ref, own_ref, blocks_ref, out_ref):
    lanes = blocks_ref.shape[0]
    total = (own_ref[...] + half_forward(spectrum_ref, blocks_ref, 1 - own_core())).T
    own = own_frequency(num_freq, lanes)
    by_real = jnp.sum(jnp.where(own, total[:num_freq], 0.0), axis=0, keepdims=True)
    by_imag = jnp.sum(jnp.where(own, total[num_freq:], 0.0), axis=0, keepdims=True)
    by_real = jnp.broadcast_to(by_real, (8, lanes))
    by_imag = jnp.broadcast_to(by_imag, (8, lanes))
    swapped, first = swap_parts(by_imag, sensors)
    data = by_real + jnp.where(first, -swapped, swapped)
    out_ref[...] = data[:1]


def sum_kernel(own_ref, *refs):
    *arrived, out_ref = refs
    total = own_ref[...]
    for ref in arrived:
        total += ref[...]
    out_ref[...] = total


def other_backward_kernel(sensors, num_freq, weight_ref, blocks_ref, *refs):
    *data_refs, out_ref, left_ref = refs
    lanes = blocks_ref.shape[0]
    pieces, _, width = out_ref.shape
    data = data_refs[0][...]
    for ref in data_refs[1:]:
        data += ref[...]
    weighted = jnp.broadcast_to(data * weight_ref[...], (8, lanes)).astype(BF16).astype(F32)
    swapped, first = swap_parts(weighted, sensors)
    turned = jnp.where(first, swapped, -swapped)
    own = own_frequency(num_freq, lanes)
    left = jnp.concatenate(
        [jnp.where(own, weighted[:1], 0.0), jnp.where(own, turned[:1], 0.0)], axis=0
    ).astype(BF16)
    left_ref[...] = left
    other = 1 - own_core()
    for piece in range(pieces):
        part = blocks_ref[:, piece_columns(piece, other, width)]
        out_ref[piece] = dot(left, part, ((1,), (0,))).astype(BF16)


def own_backward_kernel(left_ref, blocks_ref, out_ref):
    pieces, _, width = out_ref.shape
    for piece in range(pieces):
        part = blocks_ref[:, piece_columns(piece, own_core(), width)]
        out_ref[piece] = dot(left_ref[...], part, ((1,), (0,)))


def joined_kernel(first_ref, arrived_ref, out_ref):
    out_ref[...] = (first_ref[...] + arrived_ref[...].astype(F32)).astype(BF16)


def final_kernel(table_ref, adjoint_ref, out_ref):
    rows = adjoint_ref.shape[1]
    adjoint = jnp.sum(adjoint_ref[...].astype(F32), axis=0)
    table = table_ref[...]
    th, tm, tl = table[:rows], table[rows : 2 * rows], table[2 * rows :]
    ah, am, al = split3(adjoint)
    left = jnp.concatenate([tl, tm, th, tm, th, th], axis=0)
    right = jnp.concatenate([ah, am, al, ah, am, ah], axis=0)
    out_ref[...] = dot(left, right, ((0,), (0,)))


def call(kernel, outs, args, spaces=None, scratch=(), cost=None):
    spaces = spaces or [VMEM] * len(args)
    return pl.pallas_call(
        kernel,
        out_shape=[jax.ShapeDtypeStruct(shape, dtype) for shape, dtype in outs],
        in_specs=spaces,
        out_specs=[VMEM] * len(outs),
        scratch_shapes=scratch,
        compiler_params=pltpu.CompilerParams(vmem_limit_bytes=16 << 20),
        cost_estimate=cost,
    )(*args)


def per_device(seafloor_motion, response_blocks, frequencies, station_of_row, noise_precision):
    num_freq, _, sensors, params = response_blocks.shape
    num_steps, width = seafloor_motion.shape
    rows = 2 * num_freq
    lanes = rows * sensors
    pieces = params // width
    blocks = response_blocks.reshape(lanes, params)
    small = (frequencies[None], seafloor_motion, station_of_row[None], noise_precision.reshape(-1, 128))
    small = tuple(pltpu.with_memory_space_constraint(x, pltpu.HBM) for x in small)
    busy = pl.CostEstimate(flops=20 * 10**9, bytes_accessed=64 << 20, transcendentals=0)
    half = pieces // 2
    cores = [[2 * place + core for place in PLACES] for core in range(2)]
    swap = [(device, device ^ 1) for device in range(pieces)]

    copies, table, weight = call(
        spectrum_kernel,
        [((half, rows, width), BF16), ((3 * rows, num_steps), BF16), ((1, lanes), F32)],
        small,
        [HBM] * len(small),
        [pltpu.VMEM(x.shape, x.dtype) for x in small] + [pltpu.SemaphoreType.DMA((len(small),))],
        busy,
    )
    spectrum = lax.all_to_all(copies, "sensor", 0, 0, axis_index_groups=cores)
    other_spectrum = lax.ppermute(spectrum, "sensor", swap)
    (own,) = call(own_forward_kernel, [((lanes, rows), F32)], (spectrum, blocks), cost=busy)
    (partial,) = call(
        functools.partial(other_forward_kernel, sensors, num_freq),
        [((1, lanes), F32)],
        (other_spectrum, own, blocks),
        cost=busy,
    )
    row = [((1, lanes), F32)]

    def partners(value, bits):
        count = lax.axis_size("param")
        return [lax.ppermute(value, "param", [(i, i ^ bit) for i in range(count)]) for bit in bits]

    some = partial
    for bits in STAGES[:-1]:
        (some,) = call(sum_kernel, row, (some, *partners(some, bits)))
    to_other, left = call(
        functools.partial(other_backward_kernel, sensors, num_freq),
        [((half, rows, width), BF16), ((rows, lanes), BF16)],
        (weight, blocks, some, *partners(some, STAGES[-1])),
        cost=busy,
    )
    arrived = lax.ppermute(to_other, "sensor", swap)
    (first,) = call(own_backward_kernel, [((half, rows, width), F32)], (left, blocks), cost=busy)
    (joined,) = call(joined_kernel, [((half, rows, width), BF16)], (first, arrived), cost=busy)
    adjoint = lax.all_to_all(joined, "sensor", 0, 0, axis_index_groups=cores)
    return call(final_kernel, [((num_steps, width), F32)], (table, adjoint))[0]


def solution(mesh):
    in_specs = (
        P(None, ("param", "sensor")),
        P(None, None, "sensor", "param"),
        P(),
        P("sensor"),
        P(),
    )
    return jax.shard_map(
        per_device,
        mesh=mesh,
        in_specs=in_specs,
        out_specs=P(None, ("param", "sensor")),
        check_vma=False,
    )
```

```python
import functools
import math

import jax
import jax.numpy as jnp
from jax import lax
from jax.experimental import pallas as pl
from jax.experimental.pallas import tpu as pltpu
from jax.sharding import PartitionSpec as P

F32 = jnp.float32
STAGES = ((1,), (3,), (4,), (12,))
PLACES = (0, 5, 2, 7, 4, 1, 6, 3)
BF16 = jnp.bfloat16
VMEM = pl.BlockSpec(memory_space=pltpu.VMEM)
HBM = pl.BlockSpec(memory_space=pltpu.HBM)
SIN_TERMS = (-1.0 / 6, 1.0 / 120, -1.0 / 5040, 1.0 / 362880, -1.0 / 39916800)
COS_TERMS = (-1.0 / 2, 1.0 / 24, -1.0 / 720, 1.0 / 40320, -1.0 / 3628800, 1.0 / 479001600)


def series(square, terms):
    total = jnp.full_like(square, terms[-1])
    for term in terms[-2::-1]:
        total = total * square + term
    return total


def trig_tables(frequency, step, num_steps):
    turns = (frequency * step).astype(F32)
    rest = turns - num_steps * jnp.floor(turns * (1.0 / num_steps))
    rest = jnp.where(rest < 0, rest + num_steps, rest)
    rest = jnp.where(rest >= num_steps, rest - num_steps, rest)
    rest = jnp.where(rest > num_steps / 2, rest - num_steps, rest)
    flip = jnp.abs(rest) > num_steps / 4
    near = jnp.where(flip, jnp.where(rest > 0, num_steps / 2, -num_steps / 2) - rest, rest)
    angle = near * (2.0 * math.pi / num_steps)
    square = angle * angle
    scale = 1.0 / math.sqrt(num_steps)
    cosine = (1.0 + square * series(square, COS_TERMS)) * jnp.where(flip, -scale, scale)
    sine = (angle + angle * square * series(square, SIN_TERMS)) * scale
    return cosine, sine


def split3(value):
    high = value.astype(BF16)
    rest = value - high.astype(F32)
    middle = rest.astype(BF16)
    low = (rest - middle.astype(F32)).astype(BF16)
    return high, middle, low


def dot(a, b, dims):
    return lax.dot_general(a, b, (dims, ((), ())), preferred_element_type=F32)


def column_of(row):
    size = row.shape[1]
    across = lax.broadcasted_iota(jnp.int32, (size, size), 1)
    down = lax.broadcasted_iota(jnp.int32, (size, size), 0)
    return jnp.sum(jnp.where(across == down, row, jnp.zeros_like(row)), axis=1, keepdims=True)


def spectrum_kernel(
    frequencies_hbm, motion_hbm, station_hbm, noise_hbm, out_ref, table_ref, weight_ref,
    frequencies_ref, motion_ref, station_ref, noise_ref, sems,
):
    copies = [
        pltpu.make_async_copy(source, target, sems.at[i])
        for i, (source, target) in enumerate(
            [
                (frequencies_hbm, frequencies_ref),
                (station_hbm, station_ref),
                (noise_hbm, noise_ref),
                (motion_hbm, motion_ref),
            ]
        )
    ]
    for copy in copies:
        copy.start()
    num_freq = frequencies_ref.shape[1]
    num_steps = motion_ref.shape[0]
    rows = 2 * num_freq

    copies[0].wait()
    frequency = column_of(frequencies_ref[...])
    step = lax.broadcasted_iota(jnp.int32, (num_freq, num_steps), 1)
    cosine, sine = trig_tables(frequency, step, num_steps)
    table = jnp.concatenate(split3(jnp.concatenate([cosine, -sine], axis=0)), axis=0)
    table_ref[...] = table

    copies[1].wait()
    copies[2].wait()
    sensors, lanes = station_ref.shape[1], weight_ref.shape[1]
    station = column_of(station_ref[...])
    runs, length = noise_ref.shape
    place = lax.broadcasted_iota(jnp.int32, (sensors, length), 1)
    found = jnp.zeros((sensors, length), F32)
    for run in range(runs):
        found += jnp.where(station == place + run * length, noise_ref[run : run + 1], 0.0)
    by_sensor = jnp.sum(found, axis=1, keepdims=True)
    sensor = lax.broadcasted_iota(jnp.int32, (sensors, lanes), 0)
    lane = lax.rem(lax.broadcasted_iota(jnp.int32, (1, lanes), 1), sensors)
    weight_ref[...] = jnp.sum(jnp.where(sensor == lane, by_sensor, 0.0), axis=0, keepdims=True)

    copies[3].wait()
    high, middle, low = split3(motion_ref[...])
    nn = ((1,), (0,))
    by_high = dot(table, high, nn)
    by_middle = dot(table[: 2 * rows], middle, nn)
    by_low = dot(table[:rows], low, nn)
    spectrum = (
        by_high[2 * rows :] + by_middle[rows:] + by_low + by_high[rows : 2 * rows] + by_middle[:rows]
    ) + by_high[:rows]
    out_ref[...] = jnp.broadcast_to(spectrum.astype(BF16)[None], out_ref.shape)


def swap_parts(row, sensors):
    lanes = row.shape[1]
    lane = lax.broadcasted_iota(jnp.int32, row.shape, 1)
    first = lax.rem(lane, 2 * sensors) < sensors
    return jnp.where(first, pltpu.roll(row, lanes - sensors, 1), pltpu.roll(row, sensors, 1)), first


def own_frequency(num_freq, lanes):
    freq = lax.broadcasted_iota(jnp.int32, (num_freq, lanes), 0)
    lane = lax.broadcasted_iota(jnp.int32, (num_freq, lanes), 1)
    each = lanes // num_freq
    return (lane >= freq * each) & (lane < (freq + 1) * each)


def own_core():
    return lax.rem(lax.axis_index("sensor"), 2)


def own_mix():
    device = lax.axis_index("sensor")
    return lax.rem(device + lax.div(device, 2), 2)


def mixed_columns(piece, mix, width):
    place = PLACES[piece]
    device = 2 * place + (1 - mix if place % 2 else mix)
    return pl.ds(pl.multiple_of(device * width, width), width)


def piece_columns(piece, core, width):
    return pl.ds(pl.multiple_of((2 * PLACES[piece] + core) * width, width), width)


def half_forward(spectrum_ref, blocks_ref, core):
    pieces, _, width = spectrum_ref.shape
    spectrum = jnp.concatenate([spectrum_ref[piece] for piece in range(pieces)], axis=1)
    columns = [blocks_ref[:, mixed_columns(piece, core, width)] for piece in range(pieces)]
    return dot(jnp.concatenate(columns, axis=1), spectrum, ((1,), (1,)))


def own_forward_kernel(spectrum_ref, blocks_ref, out_ref):
    out_ref[...] = half_forward(spectrum_ref, blocks_ref, own_mix())


def other_forward_kernel(sensors, num_freq, spectrum_ref, own_ref, blocks_ref, out_ref):
    lanes = blocks_ref.shape[0]
    total = (own_ref[...] + half_forward(spectrum_ref, blocks_ref, 1 - own_mix())).T
    own = own_frequency(num_freq, lanes)
    by_real = jnp.sum(jnp.where(own, total[:num_freq], 0.0), axis=0, keepdims=True)
    by_imag = jnp.sum(jnp.where(own, total[num_freq:], 0.0), axis=0, keepdims=True)
    by_real = jnp.broadcast_to(by_real, (8, lanes))
    by_imag = jnp.broadcast_to(by_imag, (8, lanes))
    swapped, first = swap_parts(by_imag, sensors)
    data = by_real + jnp.where(first, -swapped, swapped)
    out_ref[...] = data[:1]


def sum_kernel(own_ref, *refs):
    *arrived, out_ref = refs
    total = own_ref[...]
    for ref in arrived:
        total += ref[...]
    out_ref[...] = total


def other_backward_kernel(sensors, num_freq, weight_ref, blocks_ref, *refs):
    *data_refs, out_ref, left_ref = refs
    lanes = blocks_ref.shape[0]
    pieces, _, width = out_ref.shape
    data = data_refs[0][...]
    for ref in data_refs[1:]:
        data += ref[...]
    weighted = jnp.broadcast_to(data * weight_ref[...], (8, lanes)).astype(BF16).astype(F32)
    swapped, first = swap_parts(weighted, sensors)
    turned = jnp.where(first, swapped, -swapped)
    own = own_frequency(num_freq, lanes)
    left = jnp.concatenate(
        [jnp.where(own, weighted[:1], 0.0), jnp.where(own, turned[:1], 0.0)], axis=0
    ).astype(BF16)
    left_ref[...] = left
    other = 1 - own_core()
    for piece in range(pieces):
        part = blocks_ref[:, piece_columns(piece, other, width)]
        out_ref[piece] = dot(left, part, ((1,), (0,))).astype(BF16)


def own_backward_kernel(left_ref, blocks_ref, out_ref):
    pieces, _, width = out_ref.shape
    for piece in range(pieces):
        part = blocks_ref[:, piece_columns(piece, own_core(), width)]
        out_ref[piece] = dot(left_ref[...], part, ((1,), (0,)))


def joined_kernel(first_ref, arrived_ref, out_ref):
    out_ref[...] = (first_ref[...] + arrived_ref[...].astype(F32)).astype(BF16)


def final_kernel(table_ref, adjoint_ref, out_ref):
    rows = adjoint_ref.shape[1]
    adjoint = jnp.sum(adjoint_ref[...].astype(F32), axis=0)
    table = table_ref[...]
    th, tm, tl = table[:rows], table[rows : 2 * rows], table[2 * rows :]
    ah, am, al = split3(adjoint)
    left = jnp.concatenate([tl, tm, th, tm, th, th], axis=0)
    right = jnp.concatenate([ah, am, al, ah, am, ah], axis=0)
    out_ref[...] = dot(left, right, ((0,), (0,)))


def call(kernel, outs, args, spaces=None, scratch=(), cost=None):
    spaces = spaces or [VMEM] * len(args)
    return pl.pallas_call(
        kernel,
        out_shape=[jax.ShapeDtypeStruct(shape, dtype) for shape, dtype in outs],
        in_specs=spaces,
        out_specs=[VMEM] * len(outs),
        scratch_shapes=scratch,
        compiler_params=pltpu.CompilerParams(vmem_limit_bytes=16 << 20),
        cost_estimate=cost,
    )(*args)


def per_device(seafloor_motion, response_blocks, frequencies, station_of_row, noise_precision):
    num_freq, _, sensors, params = response_blocks.shape
    num_steps, width = seafloor_motion.shape
    rows = 2 * num_freq
    lanes = rows * sensors
    pieces = params // width
    blocks = response_blocks.reshape(lanes, params)
    small = (frequencies[None], seafloor_motion, station_of_row[None], noise_precision.reshape(-1, 128))
    small = tuple(pltpu.with_memory_space_constraint(x, pltpu.HBM) for x in small)
    busy = pl.CostEstimate(flops=20 * 10**9, bytes_accessed=64 << 20, transcendentals=0)
    half = pieces // 2
    cores = [[2 * place + core for place in PLACES] for core in range(2)]
    mixes = [[2 * place + (mix ^ (place % 2)) for place in PLACES] for mix in range(2)]
    swap = [(device, device ^ 1) for device in range(pieces)]

    copies, table, weight = call(
        spectrum_kernel,
        [((half, rows, width), BF16), ((3 * rows, num_steps), BF16), ((1, lanes), F32)],
        small,
        [HBM] * len(small),
        [pltpu.VMEM(x.shape, x.dtype) for x in small] + [pltpu.SemaphoreType.DMA((len(small),))],
        busy,
    )
    spectrum = lax.all_to_all(copies, "sensor", 0, 0, axis_index_groups=mixes)
    other_spectrum = lax.ppermute(spectrum, "sensor", swap)
    (own,) = call(own_forward_kernel, [((lanes, rows), F32)], (spectrum, blocks), cost=busy)
    (partial,) = call(
        functools.partial(other_forward_kernel, sensors, num_freq),
        [((1, lanes), F32)],
        (other_spectrum, own, blocks),
        cost=busy,
    )
    row = [((1, lanes), F32)]

    def partners(value, bits):
        count = lax.axis_size("param")
        return [lax.ppermute(value, "param", [(i, i ^ bit) for i in range(count)]) for bit in bits]

    some = partial
    for bits in STAGES[:-1]:
        (some,) = call(sum_kernel, row, (some, *partners(some, bits)))
    to_other, left = call(
        functools.partial(other_backward_kernel, sensors, num_freq),
        [((half, rows, width), BF16), ((rows, lanes), BF16)],
        (weight, blocks, some, *partners(some, STAGES[-1])),
        cost=busy,
    )
    arrived = lax.ppermute(to_other, "sensor", swap)
    (first,) = call(own_backward_kernel, [((half, rows, width), F32)], (left, blocks), cost=busy)
    (joined,) = call(joined_kernel, [((half, rows, width), BF16)], (first, arrived), cost=busy)
    adjoint = lax.all_to_all(joined, "sensor", 0, 0, axis_index_groups=cores)
    return call(final_kernel, [((num_steps, width), F32)], (table, adjoint))[0]


def solution(mesh):
    in_specs = (
        P(None, ("param", "sensor")),
        P(None, None, "sensor", "param"),
        P(),
        P("sensor"),
        P(),
    )
    return jax.shard_map(
        per_device,
        mesh=mesh,
        in_specs=in_specs,
        out_specs=P(None, ("param", "sensor")),
        check_vma=False,
    )
```

```python
import functools
import math

import jax
import jax.numpy as jnp
from jax import lax
from jax.experimental import pallas as pl
from jax.experimental.pallas import tpu as pltpu
from jax.sharding import PartitionSpec as P

F32 = jnp.float32
STAGES = ((1,), (3,), (12,), (4,))
PLACES = (0, 5, 2, 7, 4, 1, 6, 3)
BF16 = jnp.bfloat16
VMEM = pl.BlockSpec(memory_space=pltpu.VMEM)
HBM = pl.BlockSpec(memory_space=pltpu.HBM)
SIN_TERMS = (-1.0 / 6, 1.0 / 120, -1.0 / 5040, 1.0 / 362880, -1.0 / 39916800)
COS_TERMS = (-1.0 / 2, 1.0 / 24, -1.0 / 720, 1.0 / 40320, -1.0 / 3628800, 1.0 / 479001600)


def series(square, terms):
    total = jnp.full_like(square, terms[-1])
    for term in terms[-2::-1]:
        total = total * square + term
    return total


def trig_tables(frequency, step, num_steps):
    turns = (frequency * step).astype(F32)
    rest = turns - num_steps * jnp.floor(turns * (1.0 / num_steps))
    rest = jnp.where(rest < 0, rest + num_steps, rest)
    rest = jnp.where(rest >= num_steps, rest - num_steps, rest)
    rest = jnp.where(rest > num_steps / 2, rest - num_steps, rest)
    flip = jnp.abs(rest) > num_steps / 4
    near = jnp.where(flip, jnp.where(rest > 0, num_steps / 2, -num_steps / 2) - rest, rest)
    angle = near * (2.0 * math.pi / num_steps)
    square = angle * angle
    scale = 1.0 / math.sqrt(num_steps)
    cosine = (1.0 + square * series(square, COS_TERMS)) * jnp.where(flip, -scale, scale)
    sine = (angle + angle * square * series(square, SIN_TERMS)) * scale
    return cosine, sine


def split3(value):
    high = value.astype(BF16)
    rest = value - high.astype(F32)
    middle = rest.astype(BF16)
    low = (rest - middle.astype(F32)).astype(BF16)
    return high, middle, low


def dot(a, b, dims):
    return lax.dot_general(a, b, (dims, ((), ())), preferred_element_type=F32)


def column_of(row):
    size = row.shape[1]
    across = lax.broadcasted_iota(jnp.int32, (size, size), 1)
    down = lax.broadcasted_iota(jnp.int32, (size, size), 0)
    return jnp.sum(jnp.where(across == down, row, jnp.zeros_like(row)), axis=1, keepdims=True)


def spectrum_kernel(
    frequencies_hbm, motion_hbm, station_hbm, noise_hbm, out_ref, table_ref, weight_ref,
    frequencies_ref, motion_ref, station_ref, noise_ref, sems,
):
    copies = [
        pltpu.make_async_copy(source, target, sems.at[i])
        for i, (source, target) in enumerate(
            [
                (frequencies_hbm, frequencies_ref),
                (station_hbm, station_ref),
                (noise_hbm, noise_ref),
                (motion_hbm, motion_ref),
            ]
        )
    ]
    for copy in copies:
        copy.start()
    num_freq = frequencies_ref.shape[1]
    num_steps = motion_ref.shape[0]
    rows = 2 * num_freq

    copies[0].wait()
    frequency = column_of(frequencies_ref[...])
    step = lax.broadcasted_iota(jnp.int32, (num_freq, num_steps), 1)
    cosine, sine = trig_tables(frequency, step, num_steps)
    table = jnp.concatenate(split3(jnp.concatenate([cosine, -sine], axis=0)), axis=0)
    table_ref[...] = table

    copies[1].wait()
    copies[2].wait()
    sensors, lanes = station_ref.shape[1], weight_ref.shape[1]
    station = column_of(station_ref[...])
    runs, length = noise_ref.shape
    place = lax.broadcasted_iota(jnp.int32, (sensors, length), 1)
    found = jnp.zeros((sensors, length), F32)
    for run in range(runs):
        found += jnp.where(station == place + run * length, noise_ref[run : run + 1], 0.0)
    by_sensor = jnp.sum(found, axis=1, keepdims=True)
    sensor = lax.broadcasted_iota(jnp.int32, (sensors, lanes), 0)
    lane = lax.rem(lax.broadcasted_iota(jnp.int32, (1, lanes), 1), sensors)
    weight_ref[...] = jnp.sum(jnp.where(sensor == lane, by_sensor, 0.0), axis=0, keepdims=True)

    copies[3].wait()
    high, middle, low = split3(motion_ref[...])
    nn = ((1,), (0,))
    by_high = dot(table, high, nn)
    by_middle = dot(table[: 2 * rows], middle, nn)
    by_low = dot(table[:rows], low, nn)
    spectrum = (
        by_high[2 * rows :] + by_middle[rows:] + by_low + by_high[rows : 2 * rows] + by_middle[:rows]
    ) + by_high[:rows]
    out_ref[...] = jnp.broadcast_to(spectrum.astype(BF16)[None], out_ref.shape)


def swap_parts(row, sensors):
    lanes = row.shape[1]
    lane = lax.broadcasted_iota(jnp.int32, row.shape, 1)
    first = lax.rem(lane, 2 * sensors) < sensors
    return jnp.where(first, pltpu.roll(row, lanes - sensors, 1), pltpu.roll(row, sensors, 1)), first


def own_frequency(num_freq, lanes):
    freq = lax.broadcasted_iota(jnp.int32, (num_freq, lanes), 0)
    lane = lax.broadcasted_iota(jnp.int32, (num_freq, lanes), 1)
    each = lanes // num_freq
    return (lane >= freq * each) & (lane < (freq + 1) * each)


def own_core():
    return lax.rem(lax.axis_index("sensor"), 2)


def piece_columns(piece, core, width):
    return pl.ds(pl.multiple_of((2 * PLACES[piece] + core) * width, width), width)


def half_forward(spectrum_ref, blocks_ref, core):
    pieces, _, width = spectrum_ref.shape
    spectrum = jnp.concatenate([spectrum_ref[piece] for piece in range(pieces)], axis=1)
    columns = [blocks_ref[:, piece_columns(piece, core, width)] for piece in range(pieces)]
    return dot(jnp.concatenate(columns, axis=1), spectrum, ((1,), (1,)))


def own_forward_kernel(spectrum_ref, blocks_ref, out_ref):
    out_ref[...] = half_forward(spectrum_ref, blocks_ref, own_core())


def other_forward_kernel(sensors, num_freq, spectrum_ref, own_ref, blocks_ref, out_ref):
    lanes = blocks_ref.shape[0]
    total = (own_ref[...] + half_forward(spectrum_ref, blocks_ref, 1 - own_core())).T
    own = own_frequency(num_freq, lanes)
    by_real = jnp.sum(jnp.where(own, total[:num_freq], 0.0), axis=0, keepdims=True)
    by_imag = jnp.sum(jnp.where(own, total[num_freq:], 0.0), axis=0, keepdims=True)
    by_real = jnp.broadcast_to(by_real, (8, lanes))
    by_imag = jnp.broadcast_to(by_imag, (8, lanes))
    swapped, first = swap_parts(by_imag, sensors)
    data = by_real + jnp.where(first, -swapped, swapped)
    out_ref[...] = data[:1]


def sum_kernel(own_ref, *refs):
    *arrived, out_ref = refs
    total = own_ref[...]
    for ref in arrived:
        total += ref[...]
    out_ref[...] = total


def other_backward_kernel(sensors, num_freq, weight_ref, blocks_ref, *refs):
    *data_refs, out_ref, left_ref = refs
    lanes = blocks_ref.shape[0]
    pieces, _, width = out_ref.shape
    data = data_refs[0][...]
    for ref in data_refs[1:]:
        data += ref[...]
    weighted = jnp.broadcast_to(data * weight_ref[...], (8, lanes)).astype(BF16).astype(F32)
    swapped, first = swap_parts(weighted, sensors)
    turned = jnp.where(first, swapped, -swapped)
    own = own_frequency(num_freq, lanes)
    left = jnp.concatenate(
        [jnp.where(own, weighted[:1], 0.0), jnp.where(own, turned[:1], 0.0)], axis=0
    ).astype(BF16)
    left_ref[...] = left
    other = 1 - own_core()
    for piece in range(pieces):
        part = blocks_ref[:, piece_columns(piece, other, width)]
        out_ref[piece] = dot(left, part, ((1,), (0,))).astype(BF16)


def own_backward_kernel(left_ref, blocks_ref, out_ref):
    pieces, _, width = out_ref.shape
    for piece in range(pieces):
        part = blocks_ref[:, piece_columns(piece, own_core(), width)]
        out_ref[piece] = dot(left_ref[...], part, ((1,), (0,)))


def joined_kernel(first_ref, arrived_ref, out_ref):
    out_ref[...] = (first_ref[...] + arrived_ref[...].astype(F32)).astype(BF16)


def final_kernel(table_ref, adjoint_ref, out_ref):
    rows = adjoint_ref.shape[1]
    adjoint = jnp.sum(adjoint_ref[...].astype(F32), axis=0)
    table = table_ref[...]
    th, tm, tl = table[:rows], table[rows : 2 * rows], table[2 * rows :]
    ah, am, al = split3(adjoint)
    left = jnp.concatenate([tl, tm, th, tm, th, th], axis=0)
    right = jnp.concatenate([ah, am, al, ah, am, ah], axis=0)
    out_ref[...] = dot(left, right, ((0,), (0,)))


def call(kernel, outs, args, spaces=None, scratch=(), cost=None):
    spaces = spaces or [VMEM] * len(args)
    return pl.pallas_call(
        kernel,
        out_shape=[jax.ShapeDtypeStruct(shape, dtype) for shape, dtype in outs],
        in_specs=spaces,
        out_specs=[VMEM] * len(outs),
        scratch_shapes=scratch,
        compiler_params=pltpu.CompilerParams(vmem_limit_bytes=16 << 20),
        cost_estimate=cost,
    )(*args)


def per_device(seafloor_motion, response_blocks, frequencies, station_of_row, noise_precision):
    num_freq, _, sensors, params = response_blocks.shape
    num_steps, width = seafloor_motion.shape
    rows = 2 * num_freq
    lanes = rows * sensors
    pieces = params // width
    blocks = response_blocks.reshape(lanes, params)
    small = (frequencies[None], seafloor_motion, station_of_row[None], noise_precision.reshape(-1, 128))
    small = tuple(pltpu.with_memory_space_constraint(x, pltpu.HBM) for x in small)
    busy = pl.CostEstimate(flops=20 * 10**9, bytes_accessed=64 << 20, transcendentals=0)
    half = pieces // 2
    cores = [[2 * place + core for place in PLACES] for core in range(2)]
    swap = [(device, device ^ 1) for device in range(pieces)]

    copies, table, weight = call(
        spectrum_kernel,
        [((half, rows, width), BF16), ((3 * rows, num_steps), BF16), ((1, lanes), F32)],
        small,
        [HBM] * len(small),
        [pltpu.VMEM(x.shape, x.dtype) for x in small] + [pltpu.SemaphoreType.DMA((len(small),))],
        busy,
    )
    spectrum = lax.all_to_all(copies, "sensor", 0, 0, axis_index_groups=cores)
    other_spectrum = lax.ppermute(spectrum, "sensor", swap)
    (own,) = call(own_forward_kernel, [((lanes, rows), F32)], (spectrum, blocks), cost=busy)
    (partial,) = call(
        functools.partial(other_forward_kernel, sensors, num_freq),
        [((1, lanes), F32)],
        (other_spectrum, own, blocks),
        cost=busy,
    )
    row = [((1, lanes), F32)]

    def partners(value, bits):
        count = lax.axis_size("param")
        return [lax.ppermute(value, "param", [(i, i ^ bit) for i in range(count)]) for bit in bits]

    some = partial
    for bits in STAGES[:-1]:
        (some,) = call(sum_kernel, row, (some, *partners(some, bits)))
    to_other, left = call(
        functools.partial(other_backward_kernel, sensors, num_freq),
        [((half, rows, width), BF16), ((rows, lanes), BF16)],
        (weight, blocks, some, *partners(some, STAGES[-1])),
        cost=busy,
    )
    arrived = lax.ppermute(to_other, "sensor", swap)
    (first,) = call(own_backward_kernel, [((half, rows, width), F32)], (left, blocks), cost=busy)
    (joined,) = call(joined_kernel, [((half, rows, width), BF16)], (first, arrived), cost=busy)
    adjoint = lax.all_to_all(joined, "sensor", 0, 0, axis_index_groups=cores)
    return call(final_kernel, [((num_steps, width), F32)], (table, adjoint))[0]


def solution(mesh):
    in_specs = (
        P(None, ("param", "sensor")),
        P(None, None, "sensor", "param"),
        P(),
        P("sensor"),
        P(),
    )
    return jax.shard_map(
        per_device,
        mesh=mesh,
        in_specs=in_specs,
        out_specs=P(None, ("param", "sensor")),
        check_vma=False,
    )
```
